32 devices in a mesh: grp: 2 (over y), row: 4 (over z), sub: 2 (over x), rhs: 2 (over core).
Axes of the slice: x: 2, y: 2, z: 4, core: 2. Of those that a mesh axis runs over, the one named last changes fastest.
Arguments:
- initial: float32 [128, 24576], P('rhs', ('grp', 'row', 'sub')), parts along dimension 1, as said below
- shifts: float32 [256], P(('grp', 'rhs')), parts along dimension 0, may hold values from 0.5 to 2
- send_list: int32 [16, 8], P('grp'), parts along dimension 0, may hold values from 0 to 5
- near_blocks: bfloat16 [768, 256, 256], P(('grp', 'row', 'sub')), parts along dimension 0, may hold values from -0.125 to 0.125
- near_row: int32 [768], P(('grp', 'row', 'sub')), parts along dimension 0, may hold values from 0 to 11, as said below
- near_src: int32 [768], P(('grp', 'row', 'sub')), parts along dimension 0, may hold values from 0 to 7
- far_u: bfloat16 [1536, 64, 256], P(('grp', 'row', 'sub')), parts along dimension 0, may hold values from -0.75 to 0.75
- far_v: bfloat16 [1536, 64, 256], P(('grp', 'row', 'sub')), parts along dimension 0, may hold values from -0.09375 to 0.09375
- far_row: int32 [1536], P(('grp', 'row', 'sub')), parts along dimension 0, may hold values from 0 to 11
- far_src: int32 [1536], P(('grp', 'row', 'sub')), parts along dimension 0, may hold values from 0 to 7, as said below
- far_rank: int32 [1536], P(('grp', 'row', 'sub')), parts along dimension 0, may hold values from 16 to 64
Outputs:
- second_basis: float32 [128, 24576], P('rhs', ('grp', 'row', 'sub')), parts along dimension 1
- residual: float32 [128, 24576], P('rhs', ('grp', 'row', 'sub')), parts along dimension 1
- hessenberg: float32 [4, 256], P(None, ('grp', 'rhs')), parts along dimension 1
The draws below stay inside these ranges and needn't reach their ends.
There are 2 independent parts, one for each index of `grp`. The reference program is written for one: setup_inputs(seed, part) draws one part's arguments, and reference() takes and returns one part's arrays. A program takes and returns all parts, laid end to end along the dimension named above; each array names one. Nothing has to cross between parts.
Inputs may be any that keep to these rules, and one draw needn't show every extreme that they name: `send_list`: A local cluster index of the sending owner. `near_row`: on each device, its first 12 dense blocks name every row cluster of its group once; the others follow a uniform law. `near_src`: an owner index. `far_row`: row cluster inside the holder's group. `far_src`: on each device, its first 8 low-rank blocks name every owner once; the others follow a uniform law. `far_rank`: columns of the factors beyond the rank do not count. `initial`: real starting vectors.
All inputs are finite; a program needn't handle non-finite values.
Results may differ from the reference program's by a relative error of at most 0.0047.
Values may be sent and summed in bfloat16 or wider, within the bound.
A program may use at most 128 MiB of HBM per device.

```python
import math
import jax
import jax.numpy as jnp
from jax import lax

B = 256
R = 64
NRHS = 128
NEAR_PER = 8
FAR_PER = 16
CL_DEV = 6
OWN = 8
GROUP_CL = 12
CLUSTERS = 48
NPAN = 12288
NEAR_DEV = 48
FAR_DEV = 96
NNEAR = 384
NFAR = 768
N_SUB = 2


def draw_initial(key, part):
    key = jax.random.fold_in(key, 11)
    key_base, key_rows, key_cols = jax.random.split(key, 3)
    position = jnp.arange(NPAN, dtype=jnp.float32) / NPAN
    row_scale = jnp.exp(jax.random.uniform(key_rows, (NPAN,), minval=0.0, maxval=2.3))
    col_scale = jnp.exp(jax.random.uniform(key_cols, (NRHS, 1), minval=0.0, maxval=2.3))
    base = jax.random.normal(key_base, (NRHS, NPAN))
    trend = 3.0 ** position
    return (base * trend * row_scale * col_scale).astype(jnp.float32)


def draw_near_row(key, part):
    key = jax.random.fold_in(key, 5)
    keys = jax.random.split(key, OWN)

    def per_device(device_key):
        key_head, key_rest = jax.random.split(device_key)
        head = jax.random.permutation(key_head, GROUP_CL).astype(jnp.int32)
        rest = jax.random.randint(key_rest, (NEAR_DEV - GROUP_CL,), 0, GROUP_CL).astype(jnp.int32)
        return jnp.concatenate([head, rest])
    return jax.vmap(per_device)(keys).reshape(-1)


def draw_far_src(key, part):
    key = jax.random.fold_in(key, 7)
    keys = jax.random.split(key, OWN)

    def per_device(device_key):
        key_head, key_rest = jax.random.split(device_key)
        head = jax.random.permutation(key_head, OWN).astype(jnp.int32)
        rest = jax.random.randint(key_rest, (FAR_DEV - OWN,), 0, OWN).astype(jnp.int32)
        return jnp.concatenate([head, rest])
    return jax.vmap(per_device)(keys).reshape(-1)


def plant(drawn, rng, smallest, top_value):
    place = [jax.random.randint(jax.random.fold_in(rng, axis), (), 0, length) for axis, length in enumerate(drawn.shape)]
    widest = drawn.shape.index(max(drawn.shape))
    next_to = place[:widest] + [(place[widest] + 1) % drawn.shape[widest]] + place[widest + 1:]
    return drawn.at[tuple(place)].set(smallest).at[tuple(next_to)].set(top_value)


def levels(rng, extent, cuts, low, largest):
    def one(dim, parts):
        heights = jax.random.uniform(jax.random.fold_in(jax.random.fold_in(rng, 6), dim), (parts,), jnp.float32, low / len(cuts), largest / len(cuts))
        return jnp.repeat(jnp.exp(heights), extent[dim] // parts).reshape((-1,) + (1,) * (len(extent) - dim - 1))

    level = one(*cuts[0])
    for cut in cuts[1:]:
        level = level * one(*cut)
    return level


def normal_values(own_key, dims, scale, bound, shards=(), held_as=jnp.bfloat16):
    values = jax.random.normal(own_key, dims, jnp.float32) * scale
    if len(shards) > 0:
        values = levels(own_key, dims, shards, -0.22, 0.18) * values
    return jnp.clip(values, min=-bound, max=bound).astype(held_as)


def setup_inputs(seed: int = 0, part: int = 0) -> dict:
    key_list = jax.random.split(jax.random.key(seed), 12)
    part_keys = jax.random.split(jax.random.fold_in(key_list[11], part), 12)
    initial = draw_initial(jax.random.fold_in(jax.random.fold_in(key_list[11], part), 71), part)
    shifts = jnp.clip(jnp.exp(math.log(2.0) - 1.3862944 * jax.random.uniform(part_keys[1], (NRHS,), jnp.float32) ** levels(part_keys[1], (NRHS,), ((0, 2),), -0.2, 0.2)), 0.5, 2.0)
    send_list = plant(jax.random.randint(part_keys[2], (OWN, OWN), 0, CL_DEV), jax.random.fold_in(part_keys[2], 1), 0, CL_DEV - 1).astype(jnp.int32)
    near_blocks = normal_values(part_keys[3], (NNEAR, B, B), (B * NEAR_PER) ** -0.5, 0.125, ((0, 8),))
    near_row = draw_near_row(jax.random.fold_in(jax.random.fold_in(key_list[11], part), 71), part)
    near_src = plant(jax.random.randint(part_keys[5], (NNEAR,), 0, OWN), jax.random.fold_in(part_keys[5], 1), 0, OWN - 1).astype(jnp.int32)
    far_u = normal_values(part_keys[6], (NFAR, R, B), R ** -0.5, 0.75, ((0, 8),))
    far_v = normal_values(part_keys[7], (NFAR, R, B), (B * FAR_PER) ** -0.5, 0.09375, ((0, 8),))
    far_row = plant(jax.random.randint(part_keys[8], (NFAR,), 0, GROUP_CL), jax.random.fold_in(part_keys[8], 1), 0, GROUP_CL - 1).astype(jnp.int32)
    far_src = draw_far_src(jax.random.fold_in(jax.random.fold_in(key_list[11], part), 71), part)
    far_rank = plant(jax.random.randint(part_keys[10], (NFAR,), R // 4, R + 1), jax.random.fold_in(part_keys[10], 1), R // 4, R).astype(jnp.int32)
    return {"initial": initial, "shifts": shifts, "send_list": send_list, "near_blocks": near_blocks, "near_row": near_row, "near_src": near_src, "far_u": far_u, "far_v": far_v, "far_row": far_row, "far_src": far_src, "far_rank": far_rank}


epsilon = 1e-06

def operator_apply(vector, shifts, send_list, near_blocks, near_row, near_src, far_u, far_v, far_row, far_src, far_rank):
    rounded = lax.optimization_barrier(vector.astype(jnp.bfloat16))
    panels = rounded.astype(jnp.float32).reshape(NRHS, CLUSTERS, B).transpose(1, 0, 2)
    devices = jnp.arange(OWN, dtype=jnp.int32)
    group_first = devices // N_SUB * GROUP_CL
    near_owner = near_src.reshape(OWN, NEAR_DEV)
    near_columns = near_owner * CL_DEV + send_list[near_owner, devices[:, None]]
    near_targets = near_row.reshape(OWN, NEAR_DEV) + group_first[:, None]
    far_owner = far_src.reshape(OWN, FAR_DEV)
    far_columns = far_owner * CL_DEV + send_list[far_owner, devices[:, None]]
    far_targets = far_row.reshape(OWN, FAR_DEV) + group_first[:, None]
    rank_index = jnp.arange(R, dtype=jnp.int32)

    def device_step(total, items):
        blocks, columns, targets, left_factor, right_factor, fcolumns, ftargets, franks = items
        near_y = jnp.einsum('nlc,nrc->nlr', panels[columns], blocks.astype(jnp.float32), precision=lax.Precision.HIGHEST)
        total = total.at[targets].add(near_y)
        coefficients = jnp.einsum('nlc,nkc->nlk', panels[fcolumns], right_factor.astype(jnp.float32), precision=lax.Precision.HIGHEST)
        coefficients = jnp.where(rank_index[None, None, :] < franks[:, None, None], coefficients, 0.0)
        coefficients = lax.optimization_barrier(coefficients.astype(jnp.bfloat16)).astype(jnp.float32)
        far_y = jnp.einsum('nlk,nkr->nlr', coefficients, left_factor.astype(jnp.float32), precision=lax.Precision.HIGHEST)
        total = total.at[ftargets].add(far_y)
        return (total, None)
    items = (near_blocks.reshape(OWN, NEAR_DEV, B, B), near_columns, near_targets, far_u.reshape(OWN, FAR_DEV, R, B), far_v.reshape(OWN, FAR_DEV, R, B), far_columns, far_targets, far_rank.reshape(OWN, FAR_DEV))
    total, _ = lax.scan(device_step, jnp.zeros((CLUSTERS, NRHS, B), jnp.float32), items)
    return total.transpose(1, 0, 2).reshape(NRHS, NPAN) + shifts[:, None] * vector

def column_mean(left, right):
    return lax.optimization_barrier(jnp.sum(left * right, axis=1)) / NPAN

def reference(initial, shifts, send_list, near_blocks, near_row, near_src, far_u, far_v, far_row, far_src, far_rank):
    beta = jnp.sqrt(column_mean(initial, initial) + epsilon)
    first = initial / beta[:, None]
    image = operator_apply(first, shifts, send_list, near_blocks, near_row, near_src, far_u, far_v, far_row, far_src, far_rank)
    first_coef = column_mean(first, image)
    remainder = image - first_coef[:, None] * first
    length_coef = jnp.sqrt(column_mean(remainder, remainder) + epsilon)
    second_basis = remainder / length_coef[:, None]
    image_next = operator_apply(second_basis, shifts, send_list, near_blocks, near_row, near_src, far_u, far_v, far_row, far_src, far_rank)
    cross_coef = column_mean(first, image_next)
    second_coef = column_mean(second_basis, image_next)
    residual = image_next - cross_coef[:, None] * first - second_coef[:, None] * second_basis
    hessenberg = jnp.stack([first_coef, length_coef, cross_coef, second_coef])
    return (second_basis, residual, hessenberg)
```

```python
import functools

import jax
import jax.numpy as jnp
from jax import lax
from jax.experimental import pallas as pl
from jax.experimental.pallas import tpu as pltpu
from jax.sharding import PartitionSpec as P

epsilon = 1e-06
CHUNKS = 2
UNROLL = 4
NT = (((1,), (1,)), ((), ()))
NN = (((1,), (0,)), ((), ()))


def arnoldi_kernel(
    row_count,
    sub_count,
    near_src,
    far_src,
    far_rank,
    chain,
    send_list,
    shifts_ref,
    x_ref,
    near_hbm,
    far_u_hbm,
    far_v_hbm,
    second_ref,
    resid_ref,
    hess_ref,
    near_v,
    u_v,
    v_v,
    rounded,
    staged,
    cols,
    coef,
    total,
    own_part,
    part_send,
    part_recv,
    image,
    dot_send,
    dot_recv,
    load_sem,
    col_send_sem,
    col_recv_sem,
    part_send_sem,
    part_recv_sem,
    dot_send_sem,
    dot_recv_sem,
):
    owners = row_count * sub_count
    row_index = lax.axis_index("row")
    sub_index = lax.axis_index("sub")
    me = row_index * sub_count + sub_index
    local_clusters, local_rhs, block = image.shape
    near_count = near_v.shape[0]
    far_count = u_v.shape[0]
    rank_pad = u_v.shape[1]
    blocks = near_count + far_count
    rows = local_rhs // CHUNKS
    panels = float(local_clusters * block * owners)

    def owner_id(offset):
        target = lax.rem(me + offset, owners)
        return {"row": target // sub_count, "sub": lax.rem(target, sub_count)}

    loads = [
        pltpu.make_async_copy(far_v_hbm, v_v, load_sem.at[0]),
        pltpu.make_async_copy(near_hbm, near_v, load_sem.at[1]),
        pltpu.make_async_copy(far_u_hbm, u_v, load_sem.at[2]),
    ]
    for load in loads:
        load.start()

    barrier = pltpu.get_barrier_semaphore()

    def greet(offset, carry):
        pl.semaphore_signal(
            barrier, inc=1, device_id=owner_id(offset), device_id_type=pl.DeviceIdType.MESH
        )
        return carry

    lax.fori_loop(1, owners, greet, 0)

    lanes = lax.broadcasted_iota(jnp.int32, (128, 128), 1)
    sublanes = lax.broadcasted_iota(jnp.int32, (128, 128), 0)
    diagonal = lanes == sublanes

    def to_column(line):
        return jnp.sum(jnp.where(diagonal, line, 0.0), axis=1, keepdims=True)

    def to_line(column):
        return jnp.sum(jnp.where(diagonal, column, 0.0), axis=0, keepdims=True)

    def part(chunk):
        return pl.ds(chunk * rows, rows)

    def send_columns(stage, chunk):
        def one(offset, carry):
            target = lax.rem(me + offset, owners)
            picked = send_list[me, target]
            staged[stage, chunk, offset] = rounded[stage, picked, part(chunk), :]
            pltpu.make_async_remote_copy(
                src_ref=staged.at[stage, chunk, offset],
                dst_ref=cols[stage][chunk].at[offset],
                send_sem=col_send_sem.at[stage, chunk],
                recv_sem=col_recv_sem.at[stage, chunk],
                device_id=owner_id(offset),
                device_id_type=pl.DeviceIdType.MESH,
            ).start()
            return carry

        lax.fori_loop(1, owners, one, 0)
        cols[stage][chunk][0] = rounded[stage, send_list[me, me], part(chunk), :]

    def send_dots(stage, chunk, values):
        pad = 128 - rows * len(values)
        column = jnp.concatenate(values + [jnp.zeros((pad, 1), jnp.float32)], axis=0)
        line = jnp.broadcast_to(to_line(column), (8, 128))
        dot_send[stage, chunk] = line
        dot_recv[stage, chunk, 0] = line

        def one(offset, carry):
            pltpu.make_async_remote_copy(
                src_ref=dot_send.at[stage, chunk],
                dst_ref=dot_recv.at[stage, chunk, offset],
                send_sem=dot_send_sem.at[stage, chunk],
                recv_sem=dot_recv_sem.at[stage, chunk],
                device_id=owner_id(offset),
                device_id_type=pl.DeviceIdType.MESH,
            ).start()
            return carry

        lax.fori_loop(1, owners, one, 0)

    def wait_bytes(ref, sem):
        pltpu.make_async_copy(ref, ref, sem).wait()

    def wait_dots(stage, chunk, count):
        wait_bytes(
            dot_recv.at[stage, chunk, pl.ds(1, owners - 1)], dot_recv_sem.at[stage, chunk]
        )

        def add(owner, acc):
            return acc + dot_recv[stage, chunk, lax.rem(me + owners - owner, owners)]

        line = lax.fori_loop(0, owners, add, jnp.zeros((8, 128), jnp.float32))
        column = to_column(line[0:1, :]) / panels
        return [column[k * rows : (k + 1) * rows] for k in range(count)]

    def slot_of(source):
        away = me - source
        return jnp.where(away < 0, away + owners, away)

    def apply_blocks(stage, chunk):
        held = cols[stage][chunk]
        wait_bytes(held.at[pl.ds(1, owners - 1)], col_recv_sem.at[stage, chunk])
        live = lax.broadcasted_iota(jnp.int32, (rows, rank_pad), 1)

        if stage == 0 and chunk == 0:
            loads[0].wait()

        def right_factors(step, carry):
            for j in range(UNROLL):
                n = step * UNROLL + j
                c = lax.dot_general(
                    held[slot_of(far_src[n])],
                    v_v[n],
                    NT,
                    preferred_element_type=jnp.float32,
                )
                coef[n] = jnp.where(live < far_rank[n], c, 0.0).astype(jnp.bfloat16)
            return carry

        lax.fori_loop(0, far_count // UNROLL, right_factors, 0)

        if stage == 0 and chunk == 0:
            loads[1].wait()

        def dense(step, carry):
            results = []
            for j in range(UNROLL):
                n = step * UNROLL + j
                results.append(
                    lax.dot_general(
                        held[slot_of(near_src[n])],
                        near_v[n],
                        NT,
                        preferred_element_type=jnp.float32,
                    )
                )
            for j in range(UNROLL):
                n = step * UNROLL + j
                total[n] = results[j] + total[chain[n]]
            return carry

        lax.fori_loop(0, near_count // UNROLL, dense, 0)

        if stage == 0 and chunk == 0:
            loads[2].wait()

        def left_factors(step, carry):
            results = []
            for j in range(UNROLL):
                n = step * UNROLL + j
                results.append(
                    lax.dot_general(coef[n], u_v[n], NN, preferred_element_type=jnp.float32)
                )
            for j in range(UNROLL):
                n = near_count + step * UNROLL + j
                total[n] = results[j] + total[chain[n]]
            return carry

        lax.fori_loop(0, far_count // UNROLL, left_factors, 0)

        for hop in range(1, sub_count):
            peer = lax.rem(sub_index + hop, sub_count)
            for q in range(local_clusters):
                last = chain[blocks + peer * local_clusters + q]
                part_send[stage, chunk, hop - 1, q] = total[last].astype(jnp.bfloat16)
            pltpu.make_async_remote_copy(
                src_ref=part_send.at[stage, chunk, hop - 1],
                dst_ref=part_recv.at[stage, chunk, hop - 1],
                send_sem=part_send_sem.at[stage, chunk],
                recv_sem=part_recv_sem.at[stage, chunk],
                device_id={"sub": peer},
                device_id_type=pl.DeviceIdType.MESH,
            ).start()
        for q in range(local_clusters):
            own_part[chunk, q] = total[chain[blocks + sub_index * local_clusters + q]]

    def gathered(stage, chunk, q):
        acc = own_part[chunk, q]
        for hop in range(sub_count - 1):
            acc = acc + part_recv[stage, chunk, hop, q].astype(jnp.float32)
        return acc

    def lane_sum(value):
        return jnp.sum(value, axis=1, keepdims=True)

    def span(q):
        return pl.ds(q * block, block)

    total[blocks] = jnp.zeros((rows, block), jnp.float32)
    for q in range(local_clusters):
        rounded[0, q] = x_ref[:, span(q)].astype(jnp.bfloat16)
    pl.semaphore_wait(barrier, owners - 1)
    for chunk in range(CHUNKS):
        send_columns(0, chunk)
        acc = jnp.zeros((rows, block), jnp.float32)
        for q in range(local_clusters):
            value = x_ref[part(chunk), span(q)]
            acc = acc + value * value
        send_dots(0, chunk, [lane_sum(acc)])

    for chunk in range(CHUNKS):
        apply_blocks(0, chunk)

    shift_line = jnp.concatenate(
        [shifts_ref[...], jnp.zeros((1, 128 - local_rhs), jnp.float32)], axis=1
    )
    shift_all = to_column(shift_line)
    shift = [shift_all[chunk * rows : (chunk + 1) * rows] for chunk in range(CHUNKS)]
    squares, inverse = [], []
    for chunk in range(CHUNKS):
        (mean_square,) = wait_dots(0, chunk, 1)
        inv_beta = 1.0 / jnp.sqrt(mean_square + epsilon)
        squares.append(mean_square)
        inverse.append(inv_beta)
        wait_bytes(part_recv.at[0, chunk], part_recv_sem.at[0, chunk])
        first_acc = jnp.zeros((rows, block), jnp.float32)
        self_acc = jnp.zeros((rows, block), jnp.float32)
        for q in range(local_clusters):
            value = gathered(0, chunk, q) * inv_beta
            image[q, part(chunk), :] = value
            rounded[1, q, part(chunk), :] = value.astype(jnp.bfloat16)
            first_acc = first_acc + (x_ref[part(chunk), span(q)] * inv_beta) * value
            self_acc = self_acc + value * value
        send_columns(1, chunk)
        send_dots(1, chunk, [lane_sum(first_acc), lane_sum(self_acc)])

    for chunk in range(CHUNKS):
        apply_blocks(1, chunk)

    coefficients = []
    for chunk in range(CHUNKS):
        inv_beta = inverse[chunk]
        first_image, image_square = wait_dots(1, chunk, 2)
        norm = squares[chunk] + epsilon
        first_square = squares[chunk] / norm
        drift = first_image - shift[chunk] * (epsilon / norm)
        first_coef = shift[chunk] + drift
        length = image_square - 2.0 * drift * first_image + drift * drift * first_square
        length_coef = jnp.sqrt(jnp.maximum(length, 0.0) + epsilon)
        inv_length = 1.0 / length_coef
        coefficients.append((first_coef, length_coef))
        wait_bytes(part_recv.at[1, chunk], part_recv_sem.at[1, chunk])
        first_acc = jnp.zeros((rows, block), jnp.float32)
        second_acc = jnp.zeros((rows, block), jnp.float32)
        for q in range(local_clusters):
            base = image[q, part(chunk), :]
            first = x_ref[part(chunk), span(q)] * inv_beta
            second = (base - drift * first) * inv_length
            image_next = shift[chunk] * second + (gathered(1, chunk, q) - drift * base) * inv_length
            second_ref[part(chunk), span(q)] = second
            resid_ref[part(chunk), span(q)] = image_next
            first_acc = first_acc + first * image_next
            second_acc = second_acc + second * image_next
        send_dots(2, chunk, [lane_sum(first_acc), lane_sum(second_acc)])

    table = [[], [], [], []]
    for chunk in range(CHUNKS):
        cross_coef, second_coef = wait_dots(2, chunk, 2)
        cross_first = cross_coef * inverse[chunk]
        for q in range(local_clusters):
            resid_ref[part(chunk), span(q)] = (
                resid_ref[part(chunk), span(q)]
                - cross_first * x_ref[part(chunk), span(q)]
                - second_coef * second_ref[part(chunk), span(q)]
            )
        for entry, value in zip(table, coefficients[chunk] + (cross_coef, second_coef)):
            entry.append(value)
    for k in range(4):
        column = jnp.concatenate(
            table[k] + [jnp.zeros((128 - local_rhs, 1), jnp.float32)], axis=0
        )
        hess_ref[k : k + 1, :] = to_line(column)[:, :local_rhs]

    for chunk in range(CHUNKS):
        for stage in range(2):
            wait_bytes(
                staged.at[stage, chunk, pl.ds(1, owners - 1)], col_send_sem.at[stage, chunk]
            )
            wait_bytes(part_send.at[stage, chunk], part_send_sem.at[stage, chunk])
        for stage in range(3):
            wait_bytes(
                dot_recv.at[stage, chunk, pl.ds(1, owners - 1)], dot_send_sem.at[stage, chunk]
            )


def local(
    row_count,
    sub_count,
    initial,
    shifts,
    send_list,
    near_blocks,
    near_row,
    near_src,
    far_u,
    far_v,
    far_row,
    far_src,
    far_rank,
):
    owners = row_count * sub_count
    local_rhs, width = initial.shape
    near_count, block = near_blocks.shape[:2]
    far_count, rank_pad = far_u.shape[:2]
    clusters = width // block
    blocks = near_count + far_count
    rows = local_rhs // CHUNKS

    targets = jnp.concatenate([near_row, far_row])
    wanted = jnp.concatenate([targets, jnp.arange(clusters * sub_count, dtype=jnp.int32)])
    order = jnp.arange(blocks, dtype=jnp.int32)
    place = jnp.arange(wanted.shape[0], dtype=jnp.int32)
    same = (targets[None, :] == wanted[:, None]) & (order[None, :] < place[:, None])
    chain = jnp.max(jnp.where(same, order[None, :], -1), axis=1)
    chain = jnp.where(chain < 0, blocks, chain)

    smem = pl.BlockSpec(memory_space=pltpu.SMEM)
    vmem = pl.BlockSpec(memory_space=pltpu.VMEM)
    hbm = pl.BlockSpec(memory_space=pl.ANY)
    bf16, f32 = jnp.bfloat16, jnp.float32
    return pl.pallas_call(
        functools.partial(arnoldi_kernel, row_count, sub_count),
        out_shape=(
            jax.ShapeDtypeStruct((local_rhs, width), f32),
            jax.ShapeDtypeStruct((local_rhs, width), f32),
            jax.ShapeDtypeStruct((4, local_rhs), f32),
        ),
        in_specs=[smem] * 5 + [vmem] * 2 + [hbm] * 3,
        out_specs=(vmem, vmem, vmem),
        scratch_shapes=[
            pltpu.VMEM(near_blocks.shape, bf16),
            pltpu.VMEM(far_u.shape, bf16),
            pltpu.VMEM(far_v.shape, bf16),
            pltpu.VMEM((2, clusters, local_rhs, block), bf16),
            pltpu.VMEM((2, CHUNKS, owners, rows, block), bf16),
            [[pltpu.VMEM((owners, rows, block), bf16)] * CHUNKS] * 2,
            pltpu.VMEM((far_count, rows, rank_pad), bf16),
            pltpu.VMEM((blocks + 1, rows, block), f32),
            pltpu.VMEM((CHUNKS, clusters, rows, block), f32),
            pltpu.VMEM((2, CHUNKS, sub_count - 1, clusters, rows, block), bf16),
            pltpu.VMEM((2, CHUNKS, sub_count - 1, clusters, rows, block), bf16),
            pltpu.VMEM((clusters, local_rhs, block), f32),
            pltpu.VMEM((3, CHUNKS, 8, 128), f32),
            pltpu.VMEM((3, CHUNKS, owners, 8, 128), f32),
            pltpu.SemaphoreType.DMA((3,)),
            pltpu.SemaphoreType.DMA((2, CHUNKS)),
            pltpu.SemaphoreType.DMA((2, CHUNKS)),
            pltpu.SemaphoreType.DMA((2, CHUNKS)),
            pltpu.SemaphoreType.DMA((2, CHUNKS)),
            pltpu.SemaphoreType.DMA((3, CHUNKS)),
            pltpu.SemaphoreType.DMA((3, CHUNKS)),
        ],
        compiler_params=pltpu.CompilerParams(
            collective_id=0, has_side_effects=True, vmem_limit_bytes=56 * 1024 * 1024
        ),
    )(
        near_src,
        far_src,
        far_rank,
        chain,
        send_list,
        shifts.reshape(1, local_rhs),
        initial,
        near_blocks,
        far_u,
        far_v,
    )


def solution(mesh):
    placed = (
        P("rhs", ("grp", "row", "sub")),
        P(("grp", "rhs")),
        P("grp", None),
        P(("grp", "row", "sub"), None, None),
        P(("grp", "row", "sub")),
        P(("grp", "row", "sub")),
        P(("grp", "row", "sub"), None, None),
        P(("grp", "row", "sub"), None, None),
        P(("grp", "row", "sub")),
        P(("grp", "row", "sub")),
        P(("grp", "row", "sub")),
    )
    return jax.shard_map(
        functools.partial(local, mesh.shape["row"], mesh.shape["sub"]),
        mesh=mesh,
        in_specs=placed,
        out_specs=(
            P("rhs", ("grp", "row", "sub")),
            P("rhs", ("grp", "row", "sub")),
            P(None, ("grp", "rhs")),
        ),
        check_vma=False,
    )
```

```python
import functools

import jax
import jax.numpy as jnp
from jax import lax
from jax.experimental import pallas as pl
from jax.experimental.pallas import tpu as pltpu
from jax.sharding import PartitionSpec as P

epsilon = 1e-06
CHUNKS = 2
UNROLL = 24
NT = (((1,), (1,)), ((), ()))
NN = (((1,), (0,)), ((), ()))


def arnoldi_kernel(
    row_count,
    sub_count,
    near_src,
    far_src,
    far_rank,
    chain,
    send_list,
    shifts_ref,
    x_ref,
    near_hbm,
    far_u_hbm,
    far_v_hbm,
    second_ref,
    resid_ref,
    hess_ref,
    near_v,
    u_v,
    v_v,
    rounded,
    staged,
    cols,
    coef,
    total,
    own_part,
    part_send,
    part_recv,
    image,
    dot_send,
    dot_recv,
    load_sem,
    col_send_sem,
    col_recv_sem,
    part_send_sem,
    part_recv_sem,
    dot_send_sem,
    dot_recv_sem,
):
    owners = row_count * sub_count
    row_index = lax.axis_index("row")
    sub_index = lax.axis_index("sub")
    me = row_index * sub_count + sub_index
    local_clusters, local_rhs, block = image.shape
    near_count = near_v.shape[0]
    far_count = u_v.shape[0]
    rank_pad = u_v.shape[1]
    blocks = near_count + far_count
    rows = local_rhs // CHUNKS
    panels = float(local_clusters * block * owners)

    def owner_id(offset):
        target = lax.rem(me + offset, owners)
        return {"row": target // sub_count, "sub": lax.rem(target, sub_count)}

    loads = [
        pltpu.make_async_copy(far_v_hbm, v_v, load_sem.at[0]),
        pltpu.make_async_copy(near_hbm, near_v, load_sem.at[1]),
        pltpu.make_async_copy(far_u_hbm, u_v, load_sem.at[2]),
    ]
    for load in loads:
        load.start()

    barrier = pltpu.get_barrier_semaphore()

    def greet(offset, carry):
        pl.semaphore_signal(
            barrier, inc=1, device_id=owner_id(offset), device_id_type=pl.DeviceIdType.MESH
        )
        return carry

    lax.fori_loop(1, owners, greet, 0)

    lanes = lax.broadcasted_iota(jnp.int32, (128, 128), 1)
    sublanes = lax.broadcasted_iota(jnp.int32, (128, 128), 0)
    diagonal = lanes == sublanes

    def to_column(line):
        return jnp.sum(jnp.where(diagonal, line, 0.0), axis=1, keepdims=True)

    def to_line(column):
        return jnp.sum(jnp.where(diagonal, column, 0.0), axis=0, keepdims=True)

    def part(chunk):
        return pl.ds(chunk * rows, rows)

    def send_columns(stage, chunk):
        def one(offset, carry):
            target = lax.rem(me + offset, owners)
            picked = send_list[me, target]
            staged[stage, chunk, offset] = rounded[stage, picked, part(chunk), :]
            pltpu.make_async_remote_copy(
                src_ref=staged.at[stage, chunk, offset],
                dst_ref=cols[stage][chunk].at[offset],
                send_sem=col_send_sem.at[stage, chunk],
                recv_sem=col_recv_sem.at[stage, chunk],
                device_id=owner_id(offset),
                device_id_type=pl.DeviceIdType.MESH,
            ).start()
            return carry

        lax.fori_loop(1, owners, one, 0)
        cols[stage][chunk][0] = rounded[stage, send_list[me, me], part(chunk), :]

    def send_dots(stage, chunk, values):
        pad = 128 - rows * len(values)
        column = jnp.concatenate(values + [jnp.zeros((pad, 1), jnp.float32)], axis=0)
        line = jnp.broadcast_to(to_line(column), (8, 128))
        dot_send[stage, chunk] = line
        dot_recv[stage, chunk, 0] = line

        def one(offset, carry):
            pltpu.make_async_remote_copy(
                src_ref=dot_send.at[stage, chunk],
                dst_ref=dot_recv.at[stage, chunk, offset],
                send_sem=dot_send_sem.at[stage, chunk],
                recv_sem=dot_recv_sem.at[stage, chunk],
                device_id=owner_id(offset),
                device_id_type=pl.DeviceIdType.MESH,
            ).start()
            return carry

        lax.fori_loop(1, owners, one, 0)

    def wait_bytes(ref, sem):
        pltpu.make_async_copy(ref, ref, sem).wait()

    def wait_dots(stage, chunk, count):
        wait_bytes(
            dot_recv.at[stage, chunk, pl.ds(1, owners - 1)], dot_recv_sem.at[stage, chunk]
        )

        def add(owner, acc):
            return acc + dot_recv[stage, chunk, lax.rem(me + owners - owner, owners)]

        line = lax.fori_loop(0, owners, add, jnp.zeros((8, 128), jnp.float32))
        column = to_column(line[0:1, :]) / panels
        return [column[k * rows : (k + 1) * rows] for k in range(count)]

    def slot_of(source):
        away = me - source
        return jnp.where(away < 0, away + owners, away)

    def apply_blocks(stage, chunk):
        held = cols[stage][chunk]
        wait_bytes(held.at[pl.ds(1, owners - 1)], col_recv_sem.at[stage, chunk])
        live = lax.broadcasted_iota(jnp.int32, (rows, rank_pad), 1)

        if stage == 0 and chunk == 0:
            loads[0].wait()

        def right_factors(step, carry):
            for j in range(UNROLL):
                n = step * UNROLL + j
                c = lax.dot_general(
                    held[slot_of(far_src[n])],
                    v_v[n],
                    NT,
                    preferred_element_type=jnp.float32,
                )
                coef[n] = jnp.where(live < far_rank[n], c, 0.0).astype(jnp.bfloat16)
            return carry

        lax.fori_loop(0, far_count // UNROLL, right_factors, 0)

        if stage == 0 and chunk == 0:
            loads[1].wait()

        def dense(step, carry):
            results = []
            for j in range(UNROLL):
                n = step * UNROLL + j
                results.append(
                    lax.dot_general(
                        held[slot_of(near_src[n])],
                        near_v[n],
                        NT,
                        preferred_element_type=jnp.float32,
                    )
                )
            for j in range(UNROLL):
                n = step * UNROLL + j
                total[n] = results[j] + total[chain[n]]
            return carry

        lax.fori_loop(0, near_count // UNROLL, dense, 0)

        if stage == 0 and chunk == 0:
            loads[2].wait()

        def left_factors(step, carry):
            results = []
            for j in range(UNROLL):
                n = step * UNROLL + j
                results.append(
                    lax.dot_general(coef[n], u_v[n], NN, preferred_element_type=jnp.float32)
                )
            for j in range(UNROLL):
                n = near_count + step * UNROLL + j
                total[n] = results[j] + total[chain[n]]
            return carry

        lax.fori_loop(0, far_count // UNROLL, left_factors, 0)

        for hop in range(1, sub_count):
            peer = lax.rem(sub_index + hop, sub_count)
            for q in range(local_clusters):
                last = chain[blocks + peer * local_clusters + q]
                part_send[stage, chunk, hop - 1, q] = total[last].astype(jnp.bfloat16)
            pltpu.make_async_remote_copy(
                src_ref=part_send.at[stage, chunk, hop - 1],
                dst_ref=part_recv.at[stage, chunk, hop - 1],
                send_sem=part_send_sem.at[stage, chunk],
                recv_sem=part_recv_sem.at[stage, chunk],
                device_id={"sub": peer},
                device_id_type=pl.DeviceIdType.MESH,
            ).start()
        for q in range(local_clusters):
            own_part[chunk, q] = total[chain[blocks + sub_index * local_clusters + q]]

    def gathered(stage, chunk, q):
        acc = own_part[chunk, q]
        for hop in range(sub_count - 1):
            acc = acc + part_recv[stage, chunk, hop, q].astype(jnp.float32)
        return acc

    def lane_sum(value):
        return jnp.sum(value, axis=1, keepdims=True)

    def span(q):
        return pl.ds(q * block, block)

    total[blocks] = jnp.zeros((rows, block), jnp.float32)
    for q in range(local_clusters):
        rounded[0, q] = x_ref[:, span(q)].astype(jnp.bfloat16)
    pl.semaphore_wait(barrier, owners - 1)
    for chunk in range(CHUNKS):
        send_columns(0, chunk)
        acc = jnp.zeros((rows, block), jnp.float32)
        for q in range(local_clusters):
            value = x_ref[part(chunk), span(q)]
            acc = acc + value * value
        send_dots(0, chunk, [lane_sum(acc)])

    for chunk in range(CHUNKS):
        apply_blocks(0, chunk)

    shift_line = jnp.concatenate(
        [shifts_ref[...], jnp.zeros((1, 128 - local_rhs), jnp.float32)], axis=1
    )
    shift_all = to_column(shift_line)
    shift = [shift_all[chunk * rows : (chunk + 1) * rows] for chunk in range(CHUNKS)]
    squares, inverse = [], []
    for chunk in range(CHUNKS):
        (mean_square,) = wait_dots(0, chunk, 1)
        inv_beta = 1.0 / jnp.sqrt(mean_square + epsilon)
        squares.append(mean_square)
        inverse.append(inv_beta)
        wait_bytes(part_recv.at[0, chunk], part_recv_sem.at[0, chunk])
        first_acc = jnp.zeros((rows, block), jnp.float32)
        self_acc = jnp.zeros((rows, block), jnp.float32)
        for q in range(local_clusters):
            value = gathered(0, chunk, q) * inv_beta
            image[q, part(chunk), :] = value
            rounded[1, q, part(chunk), :] = value.astype(jnp.bfloat16)
            first_acc = first_acc + (x_ref[part(chunk), span(q)] * inv_beta) * value
            self_acc = self_acc + value * value
        send_columns(1, chunk)
        send_dots(1, chunk, [lane_sum(first_acc), lane_sum(self_acc)])

    for chunk in range(CHUNKS):
        apply_blocks(1, chunk)

    coefficients = []
    for chunk in range(CHUNKS):
        inv_beta = inverse[chunk]
        first_image, image_square = wait_dots(1, chunk, 2)
        norm = squares[chunk] + epsilon
        first_square = squares[chunk] / norm
        drift = first_image - shift[chunk] * (epsilon / norm)
        first_coef = shift[chunk] + drift
        length = image_square - 2.0 * drift * first_image + drift * drift * first_square
        length_coef = jnp.sqrt(jnp.maximum(length, 0.0) + epsilon)
        inv_length = 1.0 / length_coef
        coefficients.append((first_coef, length_coef))
        wait_bytes(part_recv.at[1, chunk], part_recv_sem.at[1, chunk])
        first_acc = jnp.zeros((rows, block), jnp.float32)
        second_acc = jnp.zeros((rows, block), jnp.float32)
        for q in range(local_clusters):
            base = image[q, part(chunk), :]
            first = x_ref[part(chunk), span(q)] * inv_beta
            second = (base - drift * first) * inv_length
            image_next = shift[chunk] * second + (gathered(1, chunk, q) - drift * base) * inv_length
            second_ref[part(chunk), span(q)] = second
            resid_ref[part(chunk), span(q)] = image_next
            first_acc = first_acc + first * image_next
            second_acc = second_acc + second * image_next
        send_dots(2, chunk, [lane_sum(first_acc), lane_sum(second_acc)])

    table = [[], [], [], []]
    for chunk in range(CHUNKS):
        cross_coef, second_coef = wait_dots(2, chunk, 2)
        cross_first = cross_coef * inverse[chunk]
        for q in range(local_clusters):
            resid_ref[part(chunk), span(q)] = (
                resid_ref[part(chunk), span(q)]
                - cross_first * x_ref[part(chunk), span(q)]
                - second_coef * second_ref[part(chunk), span(q)]
            )
        for entry, value in zip(table, coefficients[chunk] + (cross_coef, second_coef)):
            entry.append(value)
    for k in range(4):
        column = jnp.concatenate(
            table[k] + [jnp.zeros((128 - local_rhs, 1), jnp.float32)], axis=0
        )
        hess_ref[k : k + 1, :] = to_line(column)[:, :local_rhs]

    for chunk in range(CHUNKS):
        for stage in range(2):
            wait_bytes(
                staged.at[stage, chunk, pl.ds(1, owners - 1)], col_send_sem.at[stage, chunk]
            )
            wait_bytes(part_send.at[stage, chunk], part_send_sem.at[stage, chunk])
        for stage in range(3):
            wait_bytes(
                dot_recv.at[stage, chunk, pl.ds(1, owners - 1)], dot_send_sem.at[stage, chunk]
            )


def local(
    row_count,
    sub_count,
    initial,
    shifts,
    send_list,
    near_blocks,
    near_row,
    near_src,
    far_u,
    far_v,
    far_row,
    far_src,
    far_rank,
):
    owners = row_count * sub_count
    local_rhs, width = initial.shape
    near_count, block = near_blocks.shape[:2]
    far_count, rank_pad = far_u.shape[:2]
    clusters = width // block
    blocks = near_count + far_count
    rows = local_rhs // CHUNKS

    targets = jnp.concatenate([near_row, far_row])
    wanted = jnp.concatenate([targets, jnp.arange(clusters * sub_count, dtype=jnp.int32)])
    order = jnp.arange(blocks, dtype=jnp.int32)
    place = jnp.arange(wanted.shape[0], dtype=jnp.int32)
    same = (targets[None, :] == wanted[:, None]) & (order[None, :] < place[:, None])
    chain = jnp.max(jnp.where(same, order[None, :], -1), axis=1)
    chain = jnp.where(chain < 0, blocks, chain)

    smem = pl.BlockSpec(memory_space=pltpu.SMEM)
    vmem = pl.BlockSpec(memory_space=pltpu.VMEM)
    hbm = pl.BlockSpec(memory_space=pl.ANY)
    bf16, f32 = jnp.bfloat16, jnp.float32
    return pl.pallas_call(
        functools.partial(arnoldi_kernel, row_count, sub_count),
        out_shape=(
            jax.ShapeDtypeStruct((local_rhs, width), f32),
            jax.ShapeDtypeStruct((local_rhs, width), f32),
            jax.ShapeDtypeStruct((4, local_rhs), f32),
        ),
        in_specs=[smem] * 5 + [vmem] * 2 + [hbm] * 3,
        out_specs=(vmem, vmem, vmem),
        scratch_shapes=[
            pltpu.VMEM(near_blocks.shape, bf16),
            pltpu.VMEM(far_u.shape, bf16),
            pltpu.VMEM(far_v.shape, bf16),
            pltpu.VMEM((2, clusters, local_rhs, block), bf16),
            pltpu.VMEM((2, CHUNKS, owners, rows, block), bf16),
            [[pltpu.VMEM((owners, rows, block), bf16)] * CHUNKS] * 2,
            pltpu.VMEM((far_count, rows, rank_pad), bf16),
            pltpu.VMEM((blocks + 1, rows, block), f32),
            pltpu.VMEM((CHUNKS, clusters, rows, block), f32),
            pltpu.VMEM((2, CHUNKS, sub_count - 1, clusters, rows, block), bf16),
            pltpu.VMEM((2, CHUNKS, sub_count - 1, clusters, rows, block), bf16),
            pltpu.VMEM((clusters, local_rhs, block), f32),
            pltpu.VMEM((3, CHUNKS, 8, 128), f32),
            pltpu.VMEM((3, CHUNKS, owners, 8, 128), f32),
            pltpu.SemaphoreType.DMA((3,)),
            pltpu.SemaphoreType.DMA((2, CHUNKS)),
            pltpu.SemaphoreType.DMA((2, CHUNKS)),
            pltpu.SemaphoreType.DMA((2, CHUNKS)),
            pltpu.SemaphoreType.DMA((2, CHUNKS)),
            pltpu.SemaphoreType.DMA((3, CHUNKS)),
            pltpu.SemaphoreType.DMA((3, CHUNKS)),
        ],
        compiler_params=pltpu.CompilerParams(
            collective_id=0, has_side_effects=True, vmem_limit_bytes=56 * 1024 * 1024
        ),
    )(
        near_src,
        far_src,
        far_rank,
        chain,
        send_list,
        shifts.reshape(1, local_rhs),
        initial,
        near_blocks,
        far_u,
        far_v,
    )


def solution(mesh):
    placed = (
        P("rhs", ("grp", "row", "sub")),
        P(("grp", "rhs")),
        P("grp", None),
        P(("grp", "row", "sub"), None, None),
        P(("grp", "row", "sub")),
        P(("grp", "row", "sub")),
        P(("grp", "row", "sub"), None, None),
        P(("grp", "row", "sub"), None, None),
        P(("grp", "row", "sub")),
        P(("grp", "row", "sub")),
        P(("grp", "row", "sub")),
    )
    return jax.shard_map(
        functools.partial(local, mesh.shape["row"], mesh.shape["sub"]),
        mesh=mesh,
        in_specs=placed,
        out_specs=(
            P("rhs", ("grp", "row", "sub")),
            P("rhs", ("grp", "row", "sub")),
            P(None, ("grp", "rhs")),
        ),
        check_vma=False,
    )
```

```python
import functools

import jax
import jax.numpy as jnp
from jax import lax
from jax.experimental import pallas as pl
from jax.experimental.pallas import tpu as pltpu
from jax.sharding import PartitionSpec as P

epsilon = 1e-06
CHUNKS = 2
UNROLL = 24
NT = (((1,), (1,)), ((), ()))
NN = (((1,), (0,)), ((), ()))


def arnoldi_kernel(
    row_count,
    sub_count,
    near_src,
    far_src,
    far_rank,
    chain,
    send_list,
    shifts_ref,
    x_ref,
    near_hbm,
    far_u_hbm,
    far_v_hbm,
    second_ref,
    image_ref,
    table_ref,
    near_v,
    u_v,
    v_v,
    rounded,
    staged,
    cols,
    coef,
    total,
    own_part,
    part_send,
    part_recv,
    image,
    dot_send,
    dot_recv,
    load_sem,
    col_send_sem,
    col_recv_sem,
    part_send_sem,
    part_recv_sem,
    dot_send_sem,
    dot_recv_sem,
):
    owners = row_count * sub_count
    row_index = lax.axis_index("row")
    sub_index = lax.axis_index("sub")
    me = row_index * sub_count + sub_index
    local_clusters, local_rhs, block = image.shape
    near_count = near_v.shape[0]
    far_count = u_v.shape[0]
    rank_pad = u_v.shape[1]
    blocks = near_count + far_count
    rows = local_rhs // CHUNKS
    panels = float(local_clusters * block * owners)

    def owner_id(offset):
        target = lax.rem(me + offset, owners)
        return {"row": target // sub_count, "sub": lax.rem(target, sub_count)}

    loads = [
        pltpu.make_async_copy(far_v_hbm, v_v, load_sem.at[0]),
        pltpu.make_async_copy(near_hbm, near_v, load_sem.at[1]),
        pltpu.make_async_copy(far_u_hbm, u_v, load_sem.at[2]),
    ]
    for load in loads:
        load.start()

    barrier = pltpu.get_barrier_semaphore()

    def greet(offset, carry):
        pl.semaphore_signal(
            barrier, inc=1, device_id=owner_id(offset), device_id_type=pl.DeviceIdType.MESH
        )
        return carry

    lax.fori_loop(1, owners, greet, 0)

    lanes = lax.broadcasted_iota(jnp.int32, (128, 128), 1)
    sublanes = lax.broadcasted_iota(jnp.int32, (128, 128), 0)
    diagonal = lanes == sublanes

    def to_column(line):
        return jnp.sum(jnp.where(diagonal, line, 0.0), axis=1, keepdims=True)

    def to_line(column):
        return jnp.sum(jnp.where(diagonal, column, 0.0), axis=0, keepdims=True)

    def part(chunk):
        return pl.ds(chunk * rows, rows)

    def send_columns(stage, chunk):
        def one(offset, carry):
            target = lax.rem(me + offset, owners)
            picked = send_list[me, target]
            staged[stage, chunk, offset] = rounded[stage, picked, part(chunk), :]
            pltpu.make_async_remote_copy(
                src_ref=staged.at[stage, chunk, offset],
                dst_ref=cols[stage][chunk].at[offset],
                send_sem=col_send_sem.at[stage, chunk],
                recv_sem=col_recv_sem.at[stage, chunk],
                device_id=owner_id(offset),
                device_id_type=pl.DeviceIdType.MESH,
            ).start()
            return carry

        lax.fori_loop(1, owners, one, 0)
        cols[stage][chunk][0] = rounded[stage, send_list[me, me], part(chunk), :]

    def send_dots(stage, chunk, values):
        pad = 128 - rows * len(values)
        column = jnp.concatenate(values + ([jnp.zeros((pad, 1), jnp.float32)] if pad else []), axis=0)
        line = jnp.broadcast_to(to_line(column), (8, 128))
        dot_send[stage, chunk] = line
        dot_recv[stage, chunk, 0] = line

        def one(offset, carry):
            pltpu.make_async_remote_copy(
                src_ref=dot_send.at[stage, chunk],
                dst_ref=dot_recv.at[stage, chunk, offset],
                send_sem=dot_send_sem.at[stage, chunk],
                recv_sem=dot_recv_sem.at[stage, chunk],
                device_id=owner_id(offset),
                device_id_type=pl.DeviceIdType.MESH,
            ).start()
            return carry

        lax.fori_loop(1, owners, one, 0)

    def wait_bytes(ref, sem):
        pltpu.make_async_copy(ref, ref, sem).wait()

    def wait_dots(stage, chunk, count):
        wait_bytes(
            dot_recv.at[stage, chunk, pl.ds(1, owners - 1)], dot_recv_sem.at[stage, chunk]
        )

        def add(owner, acc):
            return acc + dot_recv[stage, chunk, lax.rem(me + owners - owner, owners)]

        line = lax.fori_loop(0, owners, add, jnp.zeros((8, 128), jnp.float32))
        column = to_column(line[0:1, :]) / panels
        return [column[k * rows : (k + 1) * rows] for k in range(count)]

    def slot_of(source):
        away = me - source
        return jnp.where(away < 0, away + owners, away)

    def wait_columns(stage, chunk):
        wait_bytes(cols[stage][chunk].at[pl.ds(1, owners - 1)], col_recv_sem.at[stage, chunk])

    def apply_right_and_dense(stage, chunk):
        held = cols[stage][chunk]
        live = lax.broadcasted_iota(jnp.int32, (rows, rank_pad), 1)

        if stage == 0 and chunk == 0:
            loads[0].wait()

        def right_factors(step, carry):
            for j in range(UNROLL):
                n = step * UNROLL + j
                c = lax.dot_general(
                    held[slot_of(far_src[n])],
                    v_v[n],
                    NT,
                    preferred_element_type=jnp.float32,
                )
                coef[n] = jnp.where(live < far_rank[n], c, 0.0).astype(jnp.bfloat16)
            return carry

        lax.fori_loop(0, far_count // UNROLL, right_factors, 0)

        if stage == 0 and chunk == 0:
            loads[1].wait()

        def dense(step, carry):
            results = []
            for j in range(UNROLL):
                n = step * UNROLL + j
                results.append(
                    lax.dot_general(
                        held[slot_of(near_src[n])],
                        near_v[n],
                        NT,
                        preferred_element_type=jnp.float32,
                    )
                )
            for j in range(UNROLL):
                n = step * UNROLL + j
                total[n] = results[j] + total[chain[n]]
            return carry

        lax.fori_loop(0, near_count // UNROLL, dense, 0)

    def apply_left(stage, chunk):
        if stage == 0 and chunk == 0:
            loads[2].wait()

        def left_factors(step, carry):
            results = []
            for j in range(UNROLL):
                n = step * UNROLL + j
                results.append(
                    lax.dot_general(coef[n], u_v[n], NN, preferred_element_type=jnp.float32)
                )
            for j in range(UNROLL):
                n = near_count + step * UNROLL + j
                total[n] = results[j] + total[chain[n]]
            return carry

        lax.fori_loop(0, far_count // UNROLL, left_factors, 0)

        for hop in range(1, sub_count):
            peer = lax.rem(sub_index + hop, sub_count)
            for q in range(local_clusters):
                last = chain[blocks + peer * local_clusters + q]
                part_send[stage, chunk, hop - 1, q] = total[last].astype(jnp.bfloat16)
            pltpu.make_async_remote_copy(
                src_ref=part_send.at[stage, chunk, hop - 1],
                dst_ref=part_recv.at[stage, chunk, hop - 1],
                send_sem=part_send_sem.at[stage, chunk],
                recv_sem=part_recv_sem.at[stage, chunk],
                device_id={"sub": peer},
                device_id_type=pl.DeviceIdType.MESH,
            ).start()
        for q in range(local_clusters):
            own_part[chunk, q] = total[chain[blocks + sub_index * local_clusters + q]]

    def gathered(stage, chunk, q):
        acc = own_part[chunk, q]
        for hop in range(sub_count - 1):
            acc = acc + part_recv[stage, chunk, hop, q].astype(jnp.float32)
        return acc

    def lane_sum(value):
        return jnp.sum(value, axis=1, keepdims=True)

    def span(q):
        return pl.ds(q * block, block)

    total[blocks] = jnp.zeros((rows, block), jnp.float32)
    for q in range(local_clusters):
        rounded[0, q] = x_ref[:, span(q)].astype(jnp.bfloat16)
    shift_line = jnp.concatenate(
        [shifts_ref[...], jnp.zeros((1, 128 - local_rhs), jnp.float32)], axis=1
    )
    shift_all = to_column(shift_line)
    shift = [shift_all[chunk * rows : (chunk + 1) * rows] for chunk in range(CHUNKS)]
    squares, inverse, coefficients = [], [], []
    pl.semaphore_wait(barrier, owners - 1)

    def start(chunk):
        send_columns(0, chunk)
        acc = jnp.zeros((rows, block), jnp.float32)
        for q in range(local_clusters):
            value = x_ref[part(chunk), span(q)]
            acc = acc + value * value
        send_dots(0, chunk, [lane_sum(acc)])

    def first_image_of(chunk):
        (mean_square,) = wait_dots(0, chunk, 1)
        inv_beta = 1.0 / jnp.sqrt(mean_square + epsilon)
        squares.append(mean_square)
        inverse.append(inv_beta)
        wait_bytes(part_recv.at[0, chunk], part_recv_sem.at[0, chunk])
        first_acc = jnp.zeros((rows, block), jnp.float32)
        self_acc = jnp.zeros((rows, block), jnp.float32)
        for q in range(local_clusters):
            value = gathered(0, chunk, q) * inv_beta
            image[q, part(chunk), :] = value
            rounded[1, q, part(chunk), :] = value.astype(jnp.bfloat16)
        send_columns(1, chunk)
        for q in range(local_clusters):
            value = image[q, part(chunk), :]
            first_acc = first_acc + (x_ref[part(chunk), span(q)] * inv_beta) * value
            self_acc = self_acc + value * value
        send_dots(1, chunk, [lane_sum(first_acc), lane_sum(self_acc)])

    def second_image_of(chunk):
        inv_beta = inverse[chunk]
        first_image, image_square = wait_dots(1, chunk, 2)
        norm = squares[chunk] + epsilon
        first_square = squares[chunk] / norm
        drift = first_image - shift[chunk] * (epsilon / norm)
        first_coef = shift[chunk] + drift
        length = image_square - 2.0 * drift * first_image + drift * drift * first_square
        length_coef = jnp.sqrt(jnp.maximum(length, 0.0) + epsilon)
        inv_length = 1.0 / length_coef
        coefficients.append((first_coef, length_coef))
        wait_bytes(part_recv.at[1, chunk], part_recv_sem.at[1, chunk])
        first_acc = jnp.zeros((rows, block), jnp.float32)
        second_acc = jnp.zeros((rows, block), jnp.float32)
        for q in range(local_clusters):
            base = image[q, part(chunk), :]
            first = x_ref[part(chunk), span(q)] * inv_beta
            second = (base - drift * first) * inv_length
            image_next = shift[chunk] * second + (gathered(1, chunk, q) - drift * base) * inv_length
            second_ref[part(chunk), span(q)] = second
            image_ref[part(chunk), span(q)] = image_next
            first_acc = first_acc + first * image_next
            second_acc = second_acc + second * image_next
        send_dots(2, chunk, [lane_sum(first_acc), lane_sum(second_acc)])

    start(0)
    for stage, finish in ((0, first_image_of), (1, second_image_of)):
        for chunk in range(CHUNKS):
            wait_columns(stage, chunk)
            if stage == 0 and chunk + 1 < CHUNKS:
                start(chunk + 1)
            apply_right_and_dense(stage, chunk)
            if chunk > 0:
                finish(chunk - 1)
            apply_left(stage, chunk)
        finish(CHUNKS - 1)

    table = [[], [], [], [], []]
    for chunk in range(CHUNKS):
        cross_coef, second_coef = wait_dots(2, chunk, 2)
        values = coefficients[chunk] + (cross_coef, second_coef, cross_coef * inverse[chunk])
        for entry, value in zip(table, values):
            entry.append(value)
    for k in range(5):
        column = jnp.concatenate(
            table[k] + [jnp.zeros((128 - local_rhs, 1), jnp.float32)], axis=0
        )
        table_ref[k : k + 1, :] = to_line(column)
    table_ref[5:8, :] = jnp.zeros((3, 128), jnp.float32)

    for chunk in range(CHUNKS):
        for stage in range(2):
            wait_bytes(
                staged.at[stage, chunk, pl.ds(1, owners - 1)], col_send_sem.at[stage, chunk]
            )
            wait_bytes(part_send.at[stage, chunk], part_send_sem.at[stage, chunk])
        for stage in range(3):
            wait_bytes(
                dot_recv.at[stage, chunk, pl.ds(1, owners - 1)], dot_send_sem.at[stage, chunk]
            )


def finish_kernel(second_in, image_in, table_in, x_ref, second_ref, resid_ref, hess_ref):
    rhs = x_ref.shape[0]
    shape = (128, 128)
    diagonal = lax.broadcasted_iota(jnp.int32, shape, 1) == lax.broadcasted_iota(
        jnp.int32, shape, 0
    )

    def to_column(line):
        return jnp.sum(jnp.where(diagonal, line, 0.0), axis=1, keepdims=True)[:rhs]

    second_coef = to_column(table_in[3:4, :])
    cross_first = to_column(table_in[4:5, :])
    second = second_in[...]
    second_ref[...] = second
    resid_ref[...] = image_in[...] - cross_first * x_ref[...] - second_coef * second
    hess_ref[...] = table_in[0:4, :rhs]


def local(
    row_count,
    sub_count,
    initial,
    shifts,
    send_list,
    near_blocks,
    near_row,
    near_src,
    far_u,
    far_v,
    far_row,
    far_src,
    far_rank,
):
    owners = row_count * sub_count
    local_rhs, width = initial.shape
    near_count, block = near_blocks.shape[:2]
    far_count, rank_pad = far_u.shape[:2]
    clusters = width // block
    blocks = near_count + far_count
    rows = local_rhs // CHUNKS

    targets = jnp.concatenate([near_row, far_row])
    wanted = jnp.concatenate([targets, jnp.arange(clusters * sub_count, dtype=jnp.int32)])
    order = jnp.arange(blocks, dtype=jnp.int32)
    place = jnp.arange(wanted.shape[0], dtype=jnp.int32)
    same = (targets[None, :] == wanted[:, None]) & (order[None, :] < place[:, None])
    chain = jnp.max(jnp.where(same, order[None, :], -1), axis=1)
    chain = jnp.where(chain < 0, blocks, chain)

    smem = pl.BlockSpec(memory_space=pltpu.SMEM)
    vmem = pl.BlockSpec(memory_space=pltpu.VMEM)
    hbm = pl.BlockSpec(memory_space=pl.ANY)
    bf16, f32 = jnp.bfloat16, jnp.float32
    second, image_next, table = pl.pallas_call(
        functools.partial(arnoldi_kernel, row_count, sub_count),
        out_shape=(
            jax.ShapeDtypeStruct((local_rhs, width), f32),
            jax.ShapeDtypeStruct((local_rhs, width), f32),
            jax.ShapeDtypeStruct((8, 128), f32),
        ),
        in_specs=[smem] * 5 + [vmem] * 2 + [hbm] * 3,
        out_specs=(vmem, vmem, vmem),
        scratch_shapes=[
            pltpu.VMEM(near_blocks.shape, bf16),
            pltpu.VMEM(far_u.shape, bf16),
            pltpu.VMEM(far_v.shape, bf16),
            pltpu.VMEM((2, clusters, local_rhs, block), bf16),
            pltpu.VMEM((2, CHUNKS, owners, rows, block), bf16),
            [[pltpu.VMEM((owners, rows, block), bf16)] * CHUNKS] * 2,
            pltpu.VMEM((far_count, rows, rank_pad), bf16),
            pltpu.VMEM((blocks + 1, rows, block), f32),
            pltpu.VMEM((CHUNKS, clusters, rows, block), f32),
            pltpu.VMEM((2, CHUNKS, sub_count - 1, clusters, rows, block), bf16),
            pltpu.VMEM((2, CHUNKS, sub_count - 1, clusters, rows, block), bf16),
            pltpu.VMEM((clusters, local_rhs, block), f32),
            pltpu.VMEM((3, CHUNKS, 8, 128), f32),
            pltpu.VMEM((3, CHUNKS, owners, 8, 128), f32),
            pltpu.SemaphoreType.DMA((3,)),
            pltpu.SemaphoreType.DMA((2, CHUNKS)),
            pltpu.SemaphoreType.DMA((2, CHUNKS)),
            pltpu.SemaphoreType.DMA((2, CHUNKS)),
            pltpu.SemaphoreType.DMA((2, CHUNKS)),
            pltpu.SemaphoreType.DMA((3, CHUNKS)),
            pltpu.SemaphoreType.DMA((3, CHUNKS)),
        ],
        compiler_params=pltpu.CompilerParams(
            collective_id=0, has_side_effects=True, vmem_limit_bytes=56 * 1024 * 1024
        ),
    )(
        near_src,
        far_src,
        far_rank,
        chain,
        send_list,
        shifts.reshape(1, local_rhs),
        initial,
        near_blocks,
        far_u,
        far_v,
    )
    return pl.pallas_call(
        finish_kernel,
        out_shape=(
            jax.ShapeDtypeStruct((local_rhs, width), f32),
            jax.ShapeDtypeStruct((local_rhs, width), f32),
            jax.ShapeDtypeStruct((4, local_rhs), f32),
        ),
        in_specs=[vmem] * 4,
        out_specs=(vmem, vmem, vmem),
    )(second, image_next, table, initial)


def solution(mesh):
    placed = (
        P("rhs", ("grp", "row", "sub")),
        P(("grp", "rhs")),
        P("grp", None),
        P(("grp", "row", "sub"), None, None),
        P(("grp", "row", "sub")),
        P(("grp", "row", "sub")),
        P(("grp", "row", "sub"), None, None),
        P(("grp", "row", "sub"), None, None),
        P(("grp", "row", "sub")),
        P(("grp", "row", "sub")),
        P(("grp", "row", "sub")),
    )
    return jax.shard_map(
        functools.partial(local, mesh.shape["row"], mesh.shape["sub"]),
        mesh=mesh,
        in_specs=placed,
        out_specs=(
            P("rhs", ("grp", "row", "sub")),
            P("rhs", ("grp", "row", "sub")),
            P(None, ("grp", "rhs")),
        ),
        check_vma=False,
    )
```

```python
import functools

import jax
import jax.numpy as jnp
from jax import lax
from jax.experimental import pallas as pl
from jax.experimental.pallas import tpu as pltpu
from jax.sharding import PartitionSpec as P

epsilon = 1e-06
CHUNKS = 2
UNROLL = 24
NT = (((1,), (1,)), ((), ()))
NN = (((1,), (0,)), ((), ()))


def arnoldi_kernel(
    row_count,
    sub_count,
    near_src,
    far_src,
    far_rank,
    chain,
    send_list,
    shifts_ref,
    x_ref,
    near_hbm,
    far_u_hbm,
    far_v_hbm,
    second_ref,
    image_ref,
    table_ref,
    near_v,
    u_v,
    v_v,
    rounded,
    staged,
    cols,
    coef,
    total,
    own_part,
    part_send,
    part_recv,
    image,
    dot_send,
    dot_recv,
    load_sem,
    col_send_sem,
    col_recv_sem,
    part_send_sem,
    part_recv_sem,
    dot_send_sem,
    dot_recv_sem,
):
    owners = row_count * sub_count
    row_index = lax.axis_index("row")
    sub_index = lax.axis_index("sub")
    me = row_index * sub_count + sub_index
    local_clusters, local_rhs, block = image.shape
    near_count = near_v.shape[0]
    far_count = u_v.shape[0]
    rank_pad = u_v.shape[1]
    blocks = near_count + far_count
    rows = local_rhs // CHUNKS
    panels = float(local_clusters * block * owners)

    def owner_id(offset):
        target = lax.rem(me + offset, owners)
        return {"row": target // sub_count, "sub": lax.rem(target, sub_count)}

    def each_peer(body):
        if owners <= 16:
            for offset in range(1, owners):
                body(offset)
        else:
            def step(offset, carry):
                body(offset)
                return carry

            lax.fori_loop(1, owners, step, 0)

    loads = [
        pltpu.make_async_copy(far_v_hbm, v_v, load_sem.at[0]),
        pltpu.make_async_copy(near_hbm, near_v, load_sem.at[1]),
        pltpu.make_async_copy(far_u_hbm, u_v, load_sem.at[2]),
    ]
    for load in loads:
        load.start()

    barrier = pltpu.get_barrier_semaphore()

    def greet(offset):
        pl.semaphore_signal(
            barrier, inc=1, device_id=owner_id(offset), device_id_type=pl.DeviceIdType.MESH
        )

    each_peer(greet)

    lanes = lax.broadcasted_iota(jnp.int32, (128, 128), 1)
    sublanes = lax.broadcasted_iota(jnp.int32, (128, 128), 0)
    diagonal = lanes == sublanes

    def to_column(line):
        return jnp.sum(jnp.where(diagonal, line, 0.0), axis=1, keepdims=True)

    def to_line(column):
        return jnp.sum(jnp.where(diagonal, column, 0.0), axis=0, keepdims=True)

    def part(chunk):
        return pl.ds(chunk * rows, rows)

    def send_columns(stage, chunk):
        def one(offset):
            target = lax.rem(me + offset, owners)
            picked = send_list[me, target]
            staged[stage, chunk, offset] = rounded[stage, picked, part(chunk), :]
            pltpu.make_async_remote_copy(
                src_ref=staged.at[stage, chunk, offset],
                dst_ref=cols[stage][chunk].at[offset],
                send_sem=col_send_sem.at[stage, chunk],
                recv_sem=col_recv_sem.at[stage, chunk],
                device_id=owner_id(offset),
                device_id_type=pl.DeviceIdType.MESH,
            ).start()

        each_peer(one)
        cols[stage][chunk][0] = rounded[stage, send_list[me, me], part(chunk), :]

    def send_dots(stage, values):
        pad = 128 - rows * len(values)
        column = jnp.concatenate(values + ([jnp.zeros((pad, 1), jnp.float32)] if pad else []), axis=0)
        line = jnp.broadcast_to(to_line(column), (8, 128))
        dot_send[stage] = line
        dot_recv[stage, 0] = line

        def one(offset):
            pltpu.make_async_remote_copy(
                src_ref=dot_send.at[stage],
                dst_ref=dot_recv.at[stage, offset],
                send_sem=dot_send_sem.at[stage],
                recv_sem=dot_recv_sem.at[stage],
                device_id=owner_id(offset),
                device_id_type=pl.DeviceIdType.MESH,
            ).start()

        each_peer(one)

    def wait_bytes(ref, sem):
        pltpu.make_async_copy(ref, ref, sem).wait()

    def wait_dots(stage, count):
        wait_bytes(dot_recv.at[stage, pl.ds(1, owners - 1)], dot_recv_sem.at[stage])

        def add(owner, acc):
            return acc + dot_recv[stage, lax.rem(me + owners - owner, owners)]

        line = jnp.zeros((8, 128), jnp.float32)
        if owners <= 16:
            for owner in range(owners):
                line = add(owner, line)
        else:
            line = lax.fori_loop(0, owners, add, line)
        column = to_column(line[0:1, :]) / panels
        return [column[k * rows : (k + 1) * rows] for k in range(count)]

    def slot_of(source):
        away = me - source
        return jnp.where(away < 0, away + owners, away)

    def wait_columns(stage, chunk):
        wait_bytes(cols[stage][chunk].at[pl.ds(1, owners - 1)], col_recv_sem.at[stage, chunk])

    def apply_right_and_dense(stage, chunk):
        held = cols[stage][chunk]
        live = lax.broadcasted_iota(jnp.int32, (rows, rank_pad), 1)

        if stage == 0 and chunk == 0:
            loads[0].wait()

        def right_factors(step, carry):
            for j in range(UNROLL):
                n = step * UNROLL + j
                c = lax.dot_general(
                    held[slot_of(far_src[n])],
                    v_v[n],
                    NT,
                    preferred_element_type=jnp.float32,
                )
                coef[n] = jnp.where(live < far_rank[n], c, 0.0).astype(jnp.bfloat16)
            return carry

        lax.fori_loop(0, far_count // UNROLL, right_factors, 0)

        if stage == 0 and chunk == 0:
            loads[1].wait()

        def dense(step, carry):
            results = []
            for j in range(UNROLL):
                n = step * UNROLL + j
                results.append(
                    lax.dot_general(
                        held[slot_of(near_src[n])],
                        near_v[n],
                        NT,
                        preferred_element_type=jnp.float32,
                    )
                )
            for j in range(UNROLL):
                n = step * UNROLL + j
                total[n + 1] = results[j] + total[chain[n]]
            return carry

        lax.fori_loop(0, near_count // UNROLL, dense, 0)

    def apply_left(stage, chunk):
        if stage == 0 and chunk == 0:
            loads[2].wait()

        def left_factors(step, carry):
            results = []
            for j in range(UNROLL):
                n = step * UNROLL + j
                results.append(
                    lax.dot_general(coef[n], u_v[n], NN, preferred_element_type=jnp.float32)
                )
            for j in range(UNROLL):
                n = near_count + step * UNROLL + j
                total[n + 1] = results[j] + total[chain[n]]
            return carry

        lax.fori_loop(0, far_count // UNROLL, left_factors, 0)

        for hop in range(1, sub_count):
            peer = lax.rem(sub_index + hop, sub_count)
            for q in range(local_clusters):
                last = chain[blocks + peer * local_clusters + q]
                part_send[stage, chunk, hop - 1, q] = total[last].astype(jnp.bfloat16)
            pltpu.make_async_remote_copy(
                src_ref=part_send.at[stage, chunk, hop - 1],
                dst_ref=part_recv.at[stage, chunk, hop - 1],
                send_sem=part_send_sem.at[stage, chunk],
                recv_sem=part_recv_sem.at[stage, chunk],
                device_id={"sub": peer},
                device_id_type=pl.DeviceIdType.MESH,
            ).start()
        for q in range(local_clusters):
            own_part[chunk, q] = total[chain[blocks + sub_index * local_clusters + q]]

    def gathered(stage, chunk, q):
        acc = own_part[chunk, q]
        for hop in range(sub_count - 1):
            acc = acc + part_recv[stage, chunk, hop, q].astype(jnp.float32)
        return acc

    def lane_sum(value):
        return jnp.sum(value, axis=1, keepdims=True)

    def span(q):
        return pl.ds(q * block, block)

    total[0] = jnp.zeros((rows, block), jnp.float32)
    for q in range(local_clusters):
        rounded[0, q] = x_ref[:, span(q)].astype(jnp.bfloat16)
    shift_line = jnp.concatenate(
        [shifts_ref[...], jnp.zeros((1, 128 - local_rhs), jnp.float32)], axis=1
    )
    shift_all = to_column(shift_line)
    shift = [shift_all[chunk * rows : (chunk + 1) * rows] for chunk in range(CHUNKS)]
    squares, inverse, coefficients = [], [], []
    image_dots, image_means, next_dots = [], [], []
    pl.semaphore_wait(barrier, owners - 1)

    def start_dots():
        sums = []
        for chunk in range(CHUNKS):
            acc = jnp.zeros((rows, block), jnp.float32)
            for q in range(local_clusters):
                value = x_ref[part(chunk), span(q)]
                acc = acc + value * value
            sums.append(lane_sum(acc))
        send_dots(0, sums)

    def first_image_of(chunk):
        if chunk == 0:
            squares.extend(wait_dots(0, CHUNKS))
            inverse.extend([1.0 / jnp.sqrt(value + epsilon) for value in squares])
        inv_beta = inverse[chunk]
        wait_bytes(part_recv.at[0, chunk], part_recv_sem.at[0, chunk])
        first_acc = jnp.zeros((rows, block), jnp.float32)
        self_acc = jnp.zeros((rows, block), jnp.float32)
        for q in range(local_clusters):
            value = gathered(0, chunk, q) * inv_beta
            image[q, part(chunk), :] = value
            rounded[1, q, part(chunk), :] = value.astype(jnp.bfloat16)
        send_columns(1, chunk)
        for q in range(local_clusters):
            value = image[q, part(chunk), :]
            first_acc = first_acc + (x_ref[part(chunk), span(q)] * inv_beta) * value
            self_acc = self_acc + value * value
        image_dots.extend([lane_sum(first_acc), lane_sum(self_acc)])
        if chunk == CHUNKS - 1:
            send_dots(1, image_dots)

    def second_image_of(chunk):
        inv_beta = inverse[chunk]
        if chunk == 0:
            image_means.extend(wait_dots(1, 2 * CHUNKS))
        first_image, image_square = image_means[2 * chunk : 2 * chunk + 2]
        norm = squares[chunk] + epsilon
        first_square = squares[chunk] / norm
        drift = first_image - shift[chunk] * (epsilon / norm)
        first_coef = shift[chunk] + drift
        length = image_square - 2.0 * drift * first_image + drift * drift * first_square
        length_coef = jnp.sqrt(jnp.maximum(length, 0.0) + epsilon)
        inv_length = 1.0 / length_coef
        coefficients.append((first_coef, length_coef))
        wait_bytes(part_recv.at[1, chunk], part_recv_sem.at[1, chunk])
        first_acc = jnp.zeros((rows, block), jnp.float32)
        second_acc = jnp.zeros((rows, block), jnp.float32)
        for q in range(local_clusters):
            base = image[q, part(chunk), :]
            first = x_ref[part(chunk), span(q)] * inv_beta
            second = (base - drift * first) * inv_length
            image_next = shift[chunk] * second + (gathered(1, chunk, q) - drift * base) * inv_length
            second_ref[part(chunk), span(q)] = second
            image_ref[part(chunk), span(q)] = image_next
            first_acc = first_acc + first * image_next
            second_acc = second_acc + second * image_next
        next_dots.extend([lane_sum(first_acc), lane_sum(second_acc)])
        if chunk == CHUNKS - 1:
            send_dots(2, next_dots)

    send_columns(0, 0)
    start_dots()
    for stage, finish in ((0, first_image_of), (1, second_image_of)):
        for chunk in range(CHUNKS):
            wait_columns(stage, chunk)
            if stage == 0 and chunk + 1 < CHUNKS:
                send_columns(0, chunk + 1)
            apply_right_and_dense(stage, chunk)
            if chunk > 0:
                finish(chunk - 1)
            apply_left(stage, chunk)
        finish(CHUNKS - 1)

    table = [[], [], [], [], []]
    next_means = wait_dots(2, 2 * CHUNKS)
    for chunk in range(CHUNKS):
        cross_coef, second_coef = next_means[2 * chunk : 2 * chunk + 2]
        values = coefficients[chunk] + (cross_coef, second_coef, cross_coef * inverse[chunk])
        for entry, value in zip(table, values):
            entry.append(value)
    for k in range(5):
        column = jnp.concatenate(
            table[k] + [jnp.zeros((128 - local_rhs, 1), jnp.float32)], axis=0
        )
        table_ref[k : k + 1, :] = to_line(column)
    table_ref[5:8, :] = jnp.zeros((3, 128), jnp.float32)

    for chunk in range(CHUNKS):
        for stage in range(2):
            wait_bytes(
                staged.at[stage, chunk, pl.ds(1, owners - 1)], col_send_sem.at[stage, chunk]
            )
            wait_bytes(part_send.at[stage, chunk], part_send_sem.at[stage, chunk])
    for stage in range(3):
        wait_bytes(dot_recv.at[stage, pl.ds(1, owners - 1)], dot_send_sem.at[stage])


def finish_kernel(second_in, image_in, table_in, x_ref, second_ref, resid_ref, hess_ref):
    rhs = x_ref.shape[0]
    shape = (128, 128)
    diagonal = lax.broadcasted_iota(jnp.int32, shape, 1) == lax.broadcasted_iota(
        jnp.int32, shape, 0
    )

    def to_column(line):
        return jnp.sum(jnp.where(diagonal, line, 0.0), axis=1, keepdims=True)[:rhs]

    second_coef = to_column(table_in[3:4, :])
    cross_first = to_column(table_in[4:5, :])
    second = second_in[...]
    second_ref[...] = second
    resid_ref[...] = image_in[...] - cross_first * x_ref[...] - second_coef * second
    hess_ref[...] = table_in[0:4, :rhs]


def local(
    row_count,
    sub_count,
    initial,
    shifts,
    send_list,
    near_blocks,
    near_row,
    near_src,
    far_u,
    far_v,
    far_row,
    far_src,
    far_rank,
):
    owners = row_count * sub_count
    local_rhs, width = initial.shape
    near_count, block = near_blocks.shape[:2]
    far_count, rank_pad = far_u.shape[:2]
    clusters = width // block
    blocks = near_count + far_count
    rows = local_rhs // CHUNKS

    targets = jnp.concatenate([near_row, far_row])
    wanted = jnp.concatenate([targets, jnp.arange(clusters * sub_count, dtype=jnp.int32)])
    order = jnp.arange(blocks, dtype=jnp.int32)
    place = jnp.arange(wanted.shape[0], dtype=jnp.int32)
    same = (targets[None, :] == wanted[:, None]) & (order[None, :] < place[:, None])
    chain = jnp.max(jnp.where(same, order[None, :] + 1, 0), axis=1, initial=0)

    smem = pl.BlockSpec(memory_space=pltpu.SMEM)
    vmem = pl.BlockSpec(memory_space=pltpu.VMEM)
    hbm = pl.BlockSpec(memory_space=pl.ANY)
    bf16, f32 = jnp.bfloat16, jnp.float32
    second, image_next, table = pl.pallas_call(
        functools.partial(arnoldi_kernel, row_count, sub_count),
        out_shape=(
            jax.ShapeDtypeStruct((local_rhs, width), f32),
            jax.ShapeDtypeStruct((local_rhs, width), f32),
            jax.ShapeDtypeStruct((8, 128), f32),
        ),
        in_specs=[smem] * 5 + [vmem] * 2 + [hbm] * 3,
        out_specs=(vmem, vmem, vmem),
        scratch_shapes=[
            pltpu.VMEM(near_blocks.shape, bf16),
            pltpu.VMEM(far_u.shape, bf16),
            pltpu.VMEM(far_v.shape, bf16),
            pltpu.VMEM((2, clusters, local_rhs, block), bf16),
            pltpu.VMEM((2, CHUNKS, owners, rows, block), bf16),
            [[pltpu.VMEM((owners, rows, block), bf16)] * CHUNKS] * 2,
            pltpu.VMEM((far_count, rows, rank_pad), bf16),
            pltpu.VMEM((blocks + 1, rows, block), f32),
            pltpu.VMEM((CHUNKS, clusters, rows, block), f32),
            pltpu.VMEM((2, CHUNKS, sub_count - 1, clusters, rows, block), bf16),
            pltpu.VMEM((2, CHUNKS, sub_count - 1, clusters, rows, block), bf16),
            pltpu.VMEM((clusters, local_rhs, block), f32),
            pltpu.VMEM((3, 8, 128), f32),
            pltpu.VMEM((3, owners, 8, 128), f32),
            pltpu.SemaphoreType.DMA((3,)),
            pltpu.SemaphoreType.DMA((2, CHUNKS)),
            pltpu.SemaphoreType.DMA((2, CHUNKS)),
            pltpu.SemaphoreType.DMA((2, CHUNKS)),
            pltpu.SemaphoreType.DMA((2, CHUNKS)),
            pltpu.SemaphoreType.DMA((3,)),
            pltpu.SemaphoreType.DMA((3,)),
        ],
        compiler_params=pltpu.CompilerParams(
            collective_id=0, has_side_effects=True, vmem_limit_bytes=56 * 1024 * 1024
        ),
    )(
        near_src,
        far_src,
        far_rank,
        chain,
        send_list,
        shifts.reshape(1, local_rhs),
        initial,
        near_blocks,
        far_u,
        far_v,
    )
    return pl.pallas_call(
        finish_kernel,
        out_shape=(
            jax.ShapeDtypeStruct((local_rhs, width), f32),
            jax.ShapeDtypeStruct((local_rhs, width), f32),
            jax.ShapeDtypeStruct((4, local_rhs), f32),
        ),
        in_specs=[vmem] * 4,
        out_specs=(vmem, vmem, vmem),
    )(second, image_next, table, initial)


def solution(mesh):
    placed = (
        P("rhs", ("grp", "row", "sub")),
        P(("grp", "rhs")),
        P("grp", None),
        P(("grp", "row", "sub"), None, None),
        P(("grp", "row", "sub")),
        P(("grp", "row", "sub")),
        P(("grp", "row", "sub"), None, None),
        P(("grp", "row", "sub"), None, None),
        P(("grp", "row", "sub")),
        P(("grp", "row", "sub")),
        P(("grp", "row", "sub")),
    )
    return jax.shard_map(
        functools.partial(local, mesh.shape["row"], mesh.shape["sub"]),
        mesh=mesh,
        in_specs=placed,
        out_specs=(
            P("rhs", ("grp", "row", "sub")),
            P("rhs", ("grp", "row", "sub")),
            P(None, ("grp", "rhs")),
        ),
        check_vma=False,
    )
```
